32 devices in a mesh: dp: 8 (over y, x, core), tensor: 4 (over z).
Axes of the slice: x: 2, y: 2, z: 4, core: 2. Of those that a mesh axis runs over, the one named last changes fastest.
Arguments:
- gradient: float32 [96, 512, 512], P('dp', 'tensor'), may hold values from -150 to 150
- second_moment: float32 [96, 512, 512], P('dp', 'tensor'), may hold values from 0.5 to 4
- momentum: float32 [96, 512, 512], P('dp', 'tensor'), may hold values from -6 to 6
- left_state: float32 [8, 16, 512, 512], P('dp', 'tensor'), as said below
- right_state: float32 [8, 16, 512, 512], P('dp', 'tensor'), as said below
- owner: int32 [96, 1], P('dp'), may hold values from 0 to 7; in each aligned block of 12 rows (0 to 11, 12 to 23, ...) at most 2 rows name the same one
Outputs:
- direction: float32 [96, 512, 512], P('dp', 'tensor')
- moment_new: float32 [96, 512, 512], P('dp', 'tensor')
- left_new: float32 [8, 16, 512, 512], P('dp', 'tensor')
- right_new: float32 [8, 16, 512, 512], P('dp', 'tensor')
The draws below stay inside these ranges and needn't reach their ends.
Inputs may be any that keep to these rules, and one draw needn't show every extreme that they name: Among the 12 blocks of one dp index at most 2 name the same owner, and in every draw some dp index gives exactly 2 blocks to one owner. `left_state`: each slot's matrix is symmetric positive definite. `right_state`: each slot's matrix is symmetric positive definite.
All inputs are finite; a program needn't handle non-finite values.
Results may differ from the reference program's by a relative error of at most 0.0001.
Values sent between devices are 32-bit elements; how exact they have to be, the bound alone decides.
A program may use at most 128 MiB of HBM per device.

```python
import math
import jax
import jax.numpy as jnp
import numpy as np
from jax import lax

BLOCK = 512
BLOCKS_DP = 12
PAIR_MOST = 2
NEWTON = 2
BLOCKS = 96
N_DP = 8


def draw_gradient(key, part):
    key = jax.random.fold_in(key, 11)
    keys = jax.random.split(key, 3)
    shape = (BLOCKS, BLOCK, BLOCK)
    across = jnp.arange(BLOCK, dtype=jnp.float32) / (BLOCK - 1)
    rough = jnp.exp(jax.random.uniform(keys[1], (BLOCKS, BLOCK, 1), minval=0.0, maxval=1.15))
    columns = jnp.exp(jax.random.uniform(keys[2], (BLOCKS, 1, BLOCK), minval=0.0, maxval=2.3))
    base = jnp.clip(jax.random.normal(keys[0], shape), -6.0, 6.0)
    rise = 10.0 ** (0.5 * across)
    return 0.1 * base * rise[None, :, None] * rough * columns


def positive_matrix(key, span):
    keys = jax.random.split(key, 3)
    shape = (N_DP, PAIR_MOST * N_DP, BLOCK, BLOCK)
    factor = jax.random.normal(keys[0], shape)
    gram = jnp.einsum('abij,abkj->abik', factor, factor, precision=jax.lax.Precision.HIGHEST) / BLOCK
    diagonal = jnp.exp(jax.random.uniform(keys[1], (N_DP, PAIR_MOST * N_DP, BLOCK, 1), minval=-0.69, maxval=0.69))
    rows = jnp.exp(jax.random.uniform(keys[2], (N_DP, PAIR_MOST * N_DP, BLOCK, 1), minval=0.0, maxval=0.5 * jnp.log(span)))
    eye = jnp.eye(BLOCK, dtype=jnp.float32)
    inner = 0.5 * gram + diagonal * eye
    return rows * inner * jnp.swapaxes(rows, -1, -2)


def draw_left_state(key, part):
    key = jax.random.fold_in(key, 23)
    return positive_matrix(key, 10000.0)


def draw_right_state(key, part):
    key = jax.random.fold_in(key, 37)
    return positive_matrix(key, 10000.0)


def steps_of(key, dims, cuts, smallest, high):
    def one(dim, parts):
        steps = jax.random.uniform(jax.random.fold_in(jax.random.fold_in(key, 6), dim), (parts,), jnp.float32, smallest / len(cuts), high / len(cuts))
        return jnp.repeat(jnp.exp(steps), dims[dim] // parts).reshape((-1,) + (1,) * (len(dims) - dim - 1))

    gain = one(*cuts[0])
    for cut in cuts[1:]:
        gain = gain * one(*cut)
    return gain


def routed_block(key, own, number, rows, number_of, top, bound, skew):
    ranking = jax.random.permutation(key, number_of)
    heavy_load, ordinary = portions_of(number_of, rows * top, bound, skew, True), portions_of(number_of, rows * top, bound, skew, False)
    places = jnp.arange(number_of)

    def named(sizes, offset_by):
        used = int((sizes > 0).sum())
        fixed = max(1, used // 4)
        passed = fixed + (places - fixed + offset_by * (used - fixed)) % max(1, number_of - fixed)
        return jnp.zeros((number_of,), jnp.int32).at[ranking[jnp.where(places < fixed, places, passed)]].set(jnp.asarray(sizes, jnp.int32))

    sizes = jnp.where(number % 4 == 0, named(heavy_load, number // 4), named(ordinary, number - number // 4 - 1))
    mixed = jax.random.permutation(jax.random.fold_in(own, 3), number_of)
    donor, sink = mixed[0:number_of // 2 * 2:2], mixed[1:number_of // 2 * 2:2]
    room = jnp.minimum(sizes[donor] - 1, bound - sizes[sink]) // 2
    room = jnp.where((donor == ranking[0]) | (sink == ranking[0]) | (sizes[sink] == 0), 0, jnp.maximum(room, 0))
    passed = jax.random.randint(jax.random.fold_in(own, 4), (number_of // 2,), 0, 1 << 20) % (room + 1)
    sizes = sizes.at[donor].add(-passed).at[sink].add(passed)
    items = jnp.searchsorted(jnp.cumsum(sizes), jnp.arange(rows * top), side="right").astype(jnp.int32)
    table = items.reshape(top, rows).T
    table = table[jax.random.permutation(jax.random.fold_in(own, 1), rows)]
    offset_by = jax.random.randint(jax.random.fold_in(own, 2), (rows, 1), 0, top)
    return jnp.take_along_axis(table, (jnp.arange(top)[None, :] + offset_by) % top, axis=1)


def portions_of(amount, total, reach, slope, full):
    portions = [(1 << 20) // math.isqrt(grade ** slope) + 1 for grade in range(1, amount + 1)]
    largest = reach if full else min(reach, max(-(-total // amount), total * portions[0] // sum(portions)))
    least = 1 if total - largest >= amount - 1 else 0
    given, surplus = [largest] + [least] * (amount - 1), total - largest - least * (amount - 1)
    while surplus > 0:
        movable = [i for i in range(1, amount) if given[i] < largest] or [i for i in range(1, amount) if given[i] < reach]
        pool, budget = sum([portions[i] for i in movable]), surplus
        for i in movable:
            more = min(reach - given[i], max(1, budget * portions[i] // pool), surplus)
            given[i] = given[i] + more
            surplus = surplus - more
    return np.array(given)


def normal_values(own_key, dims, scale, bound, cuts=(), kind=jnp.bfloat16):
    entries = scale * jax.random.normal(own_key, dims, jnp.float32)
    if cuts:
        entries = entries * steps_of(own_key, dims, cuts, -0.22, 0.18)
    return jnp.clip(entries, -bound, bound).astype(kind)


def setup_inputs(seed: int = 0) -> dict:
    streams_of = jax.random.split(jax.random.key(seed), 7)
    gradient = draw_gradient(jax.random.fold_in(streams_of[6], 71), 0)
    second_moment = jnp.clip(jnp.exp(math.log(4.0) - 2.0794415 * jax.random.uniform(streams_of[1], (BLOCKS, BLOCK, BLOCK), jnp.float32) ** steps_of(streams_of[1], (BLOCKS, BLOCK, BLOCK), ((0, 8), (1, 4)), -0.2, 0.2)), 0.5, 4.0)
    momentum = normal_values(streams_of[2], (BLOCKS, BLOCK, BLOCK), 1.0, 6.0, ((0, 8), (1, 4)), jnp.float32)
    left_state = draw_left_state(jax.random.fold_in(streams_of[6], 71), 0)
    right_state = draw_right_state(jax.random.fold_in(streams_of[6], 71), 0)
    owner_keys = jax.random.split(jax.random.fold_in(streams_of[5], 1), BLOCKS // BLOCKS_DP)
    owner_turns = jax.random.permutation(jax.random.fold_in(streams_of[5], 3), BLOCKS // BLOCKS_DP)
    owner = jax.vmap(lambda own, number: routed_block(jax.random.fold_in(streams_of[5], 2), own, number, BLOCKS_DP, N_DP, 1, PAIR_MOST, 2))(owner_keys, owner_turns).reshape((BLOCKS, 1))
    return {"gradient": gradient, "second_moment": second_moment, "momentum": momentum, "left_state": left_state, "right_state": right_state, "owner": owner}


factor_decay = 0.9
root_eps = 0.001
adam_decay = 0.999
adam_eps = 1e-08
momentum_decay = 0.9
mean_eps = 1e-06

def product(left, right):
    return jnp.dot(left, right, precision=lax.Precision.HIGHEST)

def inverse_root(matrix):
    eye = jnp.eye(matrix.shape[0], dtype=jnp.float32)
    shifted = matrix + root_eps * eye
    scale = jnp.sqrt(jnp.sum(shifted * shifted))
    iterate = shifted / scale
    coefficient = scale ** (-0.25)
    result = eye
    for turn in range(NEWTON):
        factor = (5.0 * eye - iterate) * 0.25
        if turn == 0:
            result = coefficient * factor
        else:
            result = product(result, factor)
        if turn + 1 < NEWTON:
            square = product(factor, factor)
            fourth = product(square, square)
            iterate = product(fourth, iterate)
    return result

def precondition(block, left_old, right_old):
    left_next = factor_decay * left_old + (1.0 - factor_decay) * product(block, block.T)
    right_next = factor_decay * right_old + (1.0 - factor_decay) * product(block.T, block)
    left_root = inverse_root(left_next)
    right_root = inverse_root(right_next)
    result = product(product(left_root, block), right_root)
    return (left_next, right_next, result)

def reference(gradient, second_moment, momentum, left_state, right_state, owner):
    slots_dp = PAIR_MOST * N_DP
    owners = owner[:, 0].reshape(N_DP, BLOCKS_DP)
    position = jnp.arange(BLOCKS_DP, dtype=jnp.int32)
    earlier = (owners[:, :, None] == owners[:, None, :]) & (position[None, None, :] < position[None, :, None])
    rank = lax.optimization_barrier(jnp.sum(earlier.astype(jnp.int32), axis=2))
    source = jnp.arange(N_DP, dtype=jnp.int32)[:, None]
    slot = (owners * slots_dp + source * PAIR_MOST + rank).reshape(-1).astype(jnp.int32)
    flat_left = left_state.reshape(N_DP * slots_dp, BLOCK, BLOCK)
    flat_right = right_state.reshape(N_DP * slots_dp, BLOCK, BLOCK)

    def one_block(index):
        where = slot[index]
        left_old = lax.dynamic_index_in_dim(flat_left, where, 0, keepdims=False)
        right_old = lax.dynamic_index_in_dim(flat_right, where, 0, keepdims=False)
        return precondition(gradient[index], left_old, right_old)
    left_done, right_done, precond = lax.map(one_block, jnp.arange(BLOCKS, dtype=jnp.int32))
    left_new = (factor_decay * flat_left).at[slot].set(left_done).reshape(left_state.shape)
    right_new = (factor_decay * flat_right).at[slot].set(right_done).reshape(right_state.shape)
    moment_new = adam_decay * second_moment + (1.0 - adam_decay) * gradient * gradient
    adam = gradient / (jnp.sqrt(moment_new) + adam_eps)
    area = float(BLOCK * BLOCK)
    adam_mean = lax.optimization_barrier(jnp.sum(adam * adam, axis=(1, 2))) / area
    pre_mean = lax.optimization_barrier(jnp.sum(precond * precond, axis=(1, 2))) / area
    ratio = jnp.sqrt(adam_mean / (pre_mean + mean_eps))
    direction = momentum_decay * momentum + ratio[:, None, None] * precond
    return (direction, moment_new, left_new, right_new)
```

```python
import functools

import jax
import jax.numpy as jnp
from jax import lax
from jax.experimental import pallas as pl
from jax.experimental.pallas import tpu as pltpu
from jax.sharding import PartitionSpec as P

PAIR_MOST = 2

factor_decay = 0.9
root_eps = 0.001
adam_decay = 0.999
adam_eps = 1e-08
momentum_decay = 0.9
mean_eps = 1e-06

MESH = pl.DeviceIdType.MESH
ROWS = 256

FOURTH = (2.44140625, -1.953125, 0.5859375, -0.078125, 0.00390625)
ROOT = (
    25.0 / 16.0,
    (-5.0 - 5.0 * FOURTH[0]) / 16.0,
    (-5.0 * FOURTH[1] + FOURTH[0]) / 16.0,
    (-5.0 * FOURTH[2] + FOURTH[1]) / 16.0,
    (-5.0 * FOURTH[3] + FOURTH[2]) / 16.0,
    (-5.0 * FOURTH[4] + FOURTH[3]) / 16.0,
    FOURTH[4] / 16.0,
)


def gather_kernel(source_ref, used_ref, gradient_ref, out_ref):
    used = used_ref[pl.program_id(0)] > 0
    out_ref[...] = jnp.where(used, gradient_ref[...], 0.0)


def gather_blocks(gradient, source, used):
    slots = source.shape[0]
    _, rows, columns = gradient.shape
    return pl.pallas_call(
        gather_kernel,
        grid_spec=pltpu.PrefetchScalarGridSpec(
            num_scalar_prefetch=2,
            grid=(slots,),
            in_specs=[pl.BlockSpec((1, rows, columns), lambda s, source, used: (source[s], 0, 0))],
            out_specs=pl.BlockSpec((1, rows, columns), lambda s, source, used: (s, 0, 0)),
        ),
        out_shape=jax.ShapeDtypeStruct((slots, rows, columns), jnp.float32),
    )(source, used, gradient)


def direction_kernel(target_ref, ratio_ref, momentum_ref, returned_ref, out_ref):
    ratio = ratio_ref[pl.program_id(0)]
    out_ref[...] = momentum_decay * momentum_ref[...] + ratio * returned_ref[...]


def directions(momentum, returned, target, ratio):
    blocks, rows, columns = momentum.shape
    return pl.pallas_call(
        direction_kernel,
        grid_spec=pltpu.PrefetchScalarGridSpec(
            num_scalar_prefetch=2,
            grid=(blocks,),
            in_specs=[
                pl.BlockSpec((1, rows, columns), lambda k, target, ratio: (k, 0, 0)),
                pl.BlockSpec((1, rows, columns), lambda k, target, ratio: (target[k], 0, 0)),
            ],
            out_specs=pl.BlockSpec((1, rows, columns), lambda k, target, ratio: (k, 0, 0)),
        ),
        out_shape=jax.ShapeDtypeStruct((blocks, rows, columns), jnp.float32),
    )(target, ratio, momentum, returned)


def halves(value):
    high = value.astype(jnp.bfloat16)
    low = (value - high.astype(jnp.float32)).astype(jnp.bfloat16)
    return high, low


def put_left(ref, rows, value):
    n = ref.shape[1] // 3
    high, low = halves(value)
    ref[rows, 0:n] = high
    ref[rows, n : 2 * n] = high
    ref[rows, 2 * n : 3 * n] = low


def put_right(ref, start, count, value):
    n = ref.shape[0] // 3
    high, low = halves(value)
    ref[pl.ds(start, count), :] = high
    ref[pl.ds(n + start, count), :] = low
    ref[pl.ds(2 * n + start, count), :] = high


def chunks(n, body):
    @pl.loop(0, n // ROWS)
    def _(index):
        start = pl.multiple_of(index * ROWS, ROWS)
        body(start, pl.ds(start, ROWS))


def dot(left, rows, right):
    return jnp.dot(left[rows, :], right[...], preferred_element_type=jnp.float32)


def eye_part(start, n):
    row = lax.broadcasted_iota(jnp.int32, (ROWS, n), 0) + start
    return row == lax.broadcasted_iota(jnp.int32, (ROWS, n), 1)


def new_factor(state, left, right, total, n):
    total[...] = jnp.zeros_like(total)

    def part(start, rows):
        value = factor_decay * state[rows, :] + (1.0 - factor_decay) * dot(left, rows, right)
        state[rows, :] = value
        shifted = value + jnp.where(eye_part(start, n), root_eps, 0.0)
        square = jnp.sum(shifted * shifted, axis=0, keepdims=True)
        total[...] += jnp.broadcast_to(jnp.sum(square, axis=1, keepdims=True), total.shape)

    chunks(n, part)


def inverse_root(state, total, left, right, one, two, emit, n):
    scale = jnp.sqrt(total[0:1, 0:1])
    coefficient = lax.rsqrt(jnp.sqrt(scale))
    inverse = 1.0 / scale

    def first(start, rows):
        value = (state[rows, :] + jnp.where(eye_part(start, n), root_eps, 0.0)) * inverse
        one[rows, :] = value
        put_left(left, rows, value)
        put_right(right, start, ROWS, value)

    chunks(n, first)

    def second(start, rows):
        two[rows, :] = dot(left, rows, right)

    chunks(n, second)

    def split_second(start, rows):
        put_right(right, start, ROWS, two[rows, :])

    chunks(n, split_second)

    def third(start, rows):
        cube = dot(left, rows, right)
        m, m2 = one[rows, :], two[rows, :]
        one[rows, :] = jnp.where(eye_part(start, n), ROOT[0], 0.0) + ROOT[1] * m + ROOT[2] * m2 + ROOT[3] * cube
        two[rows, :] = ROOT[4] * m + ROOT[5] * m2 + ROOT[6] * cube
        put_left(left, rows, cube)

    chunks(n, third)

    def split_third(start, rows):
        put_right(right, start, ROWS, two[rows, :])

    chunks(n, split_third)

    def last(start, rows):
        emit(start, rows, coefficient * (one[rows, :] + dot(left, rows, right)))

    chunks(n, last)


def step_kernel(
    n_dp, n_t, near,
    out_ref, adam_ref, left_hbm, right_hbm,
    ret_ref, adam_all, sum_all, left_out, right_out,
    stage, gbuf, lbuf, rbuf, pbuf, psum, total, one, two,
    g_left, g_right, gt_left, gt_right, w_left, w_right, x_left, x_right,
    s1, r1, s2, r2, s3, r3, s4, r4, s5, r5, lsem, rsem, losem, rosem,
):
    i = lax.axis_index("dp")
    t = lax.axis_index("tensor")
    rows = out_ref.shape[2]
    n = lbuf.shape[1]
    slots = 2 * near

    def load(index):
        return (
            pltpu.make_async_copy(left_hbm.at[index], lbuf.at[index], lsem.at[index]),
            pltpu.make_async_copy(right_hbm.at[index], rbuf.at[index], rsem.at[index]),
        )

    def save(index):
        return (
            pltpu.make_async_copy(lbuf.at[index], left_out.at[index], losem.at[index]),
            pltpu.make_async_copy(rbuf.at[index], right_out.at[index], rosem.at[index]),
        )

    barrier = pltpu.get_barrier_semaphore()
    for a in range(n_dp):
        for b in range(n_t):
            @pl.when(jnp.logical_not((i == a) & (t == b)))
            def _():
                pl.semaphore_signal(barrier, inc=1, device_id=(a, b), device_id_type=MESH)
    pl.semaphore_wait(barrier, n_dp * n_t - 1)

    def spread(r, step):
        other = lax.rem(i + step, n_dp)
        return pltpu.make_async_remote_copy(
            src_ref=out_ref.at[other, r], dst_ref=stage.at[r, i],
            send_sem=s1.at[r, step], recv_sem=r1.at[r, i],
            device_id=(other, t), device_id_type=MESH,
        )

    def forward(r, j):
        return pltpu.make_async_remote_copy(
            src_ref=stage.at[r, j], dst_ref=gbuf.at[r, lax.rem(j, near), t],
            send_sem=s2.at[r, j], recv_sem=r2.at[r, lax.rem(j, near), t],
            device_id=(i, j // near), device_id_type=MESH,
        )

    def forward_here(r, j):
        return pltpu.make_async_copy(
            stage.at[r, j], gbuf.at[r, lax.rem(j, near), t], r2.at[r, lax.rem(j, near), t]
        )

    def own(r):
        return pltpu.make_async_copy(out_ref.at[i, r], stage.at[r, i], r1.at[r, i])

    def adam_copy(step):
        return pltpu.make_async_remote_copy(
            src_ref=adam_ref, dst_ref=adam_all.at[t],
            send_sem=s5.at[step], recv_sem=r5.at[t],
            device_id=(i, lax.rem(t + step, n_t)), device_id_type=MESH,
        )

    adam_here = pltpu.make_async_copy(adam_ref, adam_all.at[t], r5.at[t])

    def home(r, b, q):
        return pltpu.make_async_remote_copy(
            src_ref=pbuf.at[r, b, pl.ds(pl.multiple_of(q * rows, rows), rows)], dst_ref=ret_ref.at[i, r],
            send_sem=s3.at[r, b, q], recv_sem=r3.at[r, i],
            device_id=(t * near + b, q), device_id_type=MESH,
        )

    def home_here(r, b, q):
        return pltpu.make_async_copy(
            pbuf.at[r, b, pl.ds(pl.multiple_of(q * rows, rows), rows)], ret_ref.at[i, r], r3.at[r, i]
        )

    def home_sum(r, b, q):
        return pltpu.make_async_remote_copy(
            src_ref=psum.at[r, b], dst_ref=sum_all.at[i, r],
            send_sem=s4.at[r, b, q], recv_sem=r4.at[r, i],
            device_id=(t * near + b, q), device_id_type=MESH,
        )

    def home_sum_here(r, b, q):
        return pltpu.make_async_copy(psum.at[r, b], sum_all.at[i, r], r4.at[r, i])

    for r in range(2):
        own(r).start()
        for step in range(1, n_dp):
            spread(r, step).start()
    adam_here.start()
    for step in range(1, n_t):
        adam_copy(step).start()
    for index in range(slots):
        for copy in load(index):
            copy.start()

    for r in range(2):
        for step in range(n_dp):
            j = lax.rem(i + n_dp - step, n_dp)
            pltpu.make_async_copy(stage.at[r, j], stage.at[r, j], r1.at[r, j]).wait()
            same = j // near == t

            @pl.when(same)
            def _():
                forward_here(r, j).start()

            @pl.when(jnp.logical_not(same))
            def _():
                forward(r, j).start()

    @pl.loop(0, slots)
    def _(q):
        r = q // near
        b = lax.rem(q, near)
        index = b * 2 + r
        for copy in load(index):
            copy.wait()
        for part in range(n_t):
            pltpu.make_async_copy(gbuf.at[r, b, part], gbuf.at[r, b, part], r2.at[r, b, part]).wait()
        left, right = lbuf.at[index], rbuf.at[index]
        for part in range(n_t):
            here = pl.ds(part * rows, rows)
            value = gbuf[r, b, part]
            put_left(g_left, here, value)
            put_right(g_right, part * rows, rows, value)
            one[here, :] = value

        def turn(start, here):
            value = jnp.transpose(one[:, here])
            put_left(gt_left, here, value)
            put_right(gt_right, start, ROWS, value)

        for start in range(0, n, ROWS):
            turn(start, pl.ds(start, ROWS))
        new_factor(left, g_left, gt_right, total.at[0], n)
        new_factor(right, gt_left, g_right, total.at[1], n)
        for copy in save(index):
            copy.start()

        def keep_left(start, here, value):
            put_left(x_left, here, value)

        def keep_right(start, here, value):
            put_right(x_right, start, ROWS, value)

        inverse_root(left, total.at[0], w_left, w_right, one, two, keep_left, n)
        inverse_root(right, total.at[1], w_left, w_right, one, two, keep_right, n)

        def middle(start, here):
            put_left(w_left, here, dot(x_left, here, g_right))

        chunks(n, middle)
        psum[r, b] = jnp.zeros(psum.shape[2:], jnp.float32)

        def final(start, here):
            value = dot(w_left, here, x_right)
            pbuf[r, b, here, :] = value
            square = jnp.sum(value * value, axis=0, keepdims=True)
            psum[r, b] += jnp.broadcast_to(jnp.sum(square, axis=1, keepdims=True), psum.shape[2:])

        chunks(n, final)
        for part in range(n_t):
            mine = (t * near + b == i) & (t == part)

            @pl.when(mine)
            def _():
                home_here(r, b, part).start()
                home_sum_here(r, b, part).start()

            @pl.when(jnp.logical_not(mine))
            def _():
                home(r, b, part).start()
                home_sum(r, b, part).start()

    for r in range(2):
        for step in range(1, n_dp):
            spread(r, step).wait_send()
        for j in range(n_dp):
            @pl.when(j // near != t)
            def _():
                forward(r, j).wait_send()
    for step in range(1, n_t):
        adam_copy(step).wait_send()
    for index in range(slots):
        for copy in save(index):
            copy.wait()
    for part in range(n_t):
        pltpu.make_async_copy(adam_all.at[part], adam_all.at[part], r5.at[part]).wait()
    for r in range(2):
        for b in range(near):
            for part in range(n_t):
                @pl.when(jnp.logical_not((t * near + b == i) & (t == part)))
                def _():
                    home(r, b, part).wait_send()
                    home_sum(r, b, part).wait_send()
        for o in range(n_dp):
            pltpu.make_async_copy(ret_ref.at[o, r], ret_ref.at[o, r], r3.at[r, o]).wait()
            pltpu.make_async_copy(sum_all.at[o, r], sum_all.at[o, r], r4.at[r, o]).wait()


def step(outgoing, adam, left_old, right_old, n_dp, n_t):
    near = n_dp // n_t
    slots = 2 * near
    _, _, rows, n = outgoing.shape
    f32, bf16 = jnp.float32, jnp.bfloat16
    vmem = pl.BlockSpec(memory_space=pltpu.VMEM)
    hbm = pl.BlockSpec(memory_space=pl.ANY)
    dma = pltpu.SemaphoreType.DMA
    wide, tall = pltpu.VMEM((n, 3 * n), bf16), pltpu.VMEM((3 * n, n), bf16)
    return pl.pallas_call(
        functools.partial(step_kernel, n_dp, n_t, near),
        out_shape=(
            jax.ShapeDtypeStruct((n_dp, 2, rows, n), f32),
            jax.ShapeDtypeStruct((n_t,) + adam.shape, f32),
            jax.ShapeDtypeStruct((n_dp, 2, 8, 128), f32),
            jax.ShapeDtypeStruct((slots, n, n), f32),
            jax.ShapeDtypeStruct((slots, n, n), f32),
        ),
        in_specs=[vmem, vmem, hbm, hbm],
        out_specs=(hbm, vmem, vmem, hbm, hbm),
        scratch_shapes=[
            pltpu.VMEM((2, n_dp, rows, n), f32),
            pltpu.VMEM((2, near, n_t, rows, n), f32),
            pltpu.VMEM((slots, n, n), f32),
            pltpu.VMEM((slots, n, n), f32),
            pltpu.VMEM((2, near, n, n), f32),
            pltpu.VMEM((2, near, 8, 128), f32),
            pltpu.VMEM((2, 8, 128), f32),
            pltpu.VMEM((n, n), f32),
            pltpu.VMEM((n, n), f32),
            wide, tall, wide, tall, wide, tall, wide, tall,
            dma((2, n_dp)), dma((2, n_dp)),
            dma((2, n_dp)), dma((2, near, n_t)),
            dma((2, near, n_t)), dma((2, n_dp)),
            dma((2, near, n_t)), dma((2, n_dp)),
            dma((n_t,)), dma((n_t,)),
            dma((slots,)), dma((slots,)), dma((slots,)), dma((slots,)),
        ],
        compiler_params=pltpu.CompilerParams(
            collective_id=0, has_side_effects=True, vmem_limit_bytes=56 * 2**20
        ),
    )(outgoing, adam, left_old, right_old)


def per_device(gradient, second_moment, momentum, left_state, right_state, owner):
    dp_count = lax.axis_size("dp")
    tensor_count = lax.axis_size("tensor")
    blocks_here, rows, columns = gradient.shape
    slots_dp = PAIR_MOST * dp_count
    owners = owner[:, 0]
    position = jnp.arange(blocks_here, dtype=jnp.int32)
    earlier = (owners[:, None] == owners[None, :]) & (position[None, :] < position[:, None])
    rank = jnp.sum(earlier.astype(jnp.int32), axis=1)
    target = owners * PAIR_MOST + rank
    select = (target[None, :] == jnp.arange(slots_dp, dtype=jnp.int32)[:, None]).astype(jnp.int32)
    source = jnp.sum(select * position[None, :], axis=1)
    used = jnp.sum(select, axis=1)
    outgoing = gather_blocks(gradient, source, used).reshape(dp_count, PAIR_MOST, rows, columns)
    moment_new = adam_decay * second_moment + (1.0 - adam_decay) * gradient * gradient
    adam = gradient / (jnp.sqrt(moment_new) + adam_eps)
    adam_part = jnp.sum(adam * adam, axis=(1, 2))
    padded = -(-blocks_here // 8) * 8
    adam_tile = jnp.broadcast_to(jnp.pad(adam_part, (0, padded - blocks_here))[:, None], (padded, 128))
    returned, adam_all, sums, left_new, right_new = step(
        outgoing, adam_tile, left_state[0], right_state[0], dp_count, tensor_count
    )
    adam_sum = jnp.sum(adam_all[:, :blocks_here, 0], axis=0)
    pre_sum = jnp.sum(
        jnp.where(select.T > 0, sums[:, :, 0, 0].reshape(1, slots_dp), 0.0), axis=1
    )
    area = float(columns * columns)
    ratio = jnp.sqrt(adam_sum / area / (pre_sum / area + mean_eps))
    direction = directions(momentum, returned.reshape(slots_dp, rows, columns), target, ratio)
    return (direction, moment_new, left_new[None], right_new[None])


def solution(mesh):
    return jax.shard_map(
        per_device,
        mesh=mesh,
        in_specs=(
            P("dp", "tensor", None),
            P("dp", "tensor", None),
            P("dp", "tensor", None),
            P("dp", "tensor", None, None),
            P("dp", "tensor", None, None),
            P("dp", None),
        ),
        out_specs=(
            P("dp", "tensor", None),
            P("dp", "tensor", None),
            P("dp", "tensor", None, None),
            P("dp", "tensor", None, None),
        ),
        check_vma=False,
    )
```

```python
import functools

import jax
import jax.numpy as jnp
from jax import lax
from jax.experimental import pallas as pl
from jax.experimental.pallas import tpu as pltpu
from jax.sharding import PartitionSpec as P

PAIR_MOST = 2

factor_decay = 0.9
root_eps = 0.001
adam_decay = 0.999
adam_eps = 1e-08
momentum_decay = 0.9
mean_eps = 1e-06

MESH = pl.DeviceIdType.MESH
ROWS = 256

FOURTH = (2.44140625, -1.953125, 0.5859375, -0.078125, 0.00390625)
ROOT = (
    25.0 / 16.0,
    (-5.0 - 5.0 * FOURTH[0]) / 16.0,
    (-5.0 * FOURTH[1] + FOURTH[0]) / 16.0,
    (-5.0 * FOURTH[2] + FOURTH[1]) / 16.0,
    (-5.0 * FOURTH[3] + FOURTH[2]) / 16.0,
    (-5.0 * FOURTH[4] + FOURTH[3]) / 16.0,
    FOURTH[4] / 16.0,
)


def gather_kernel(source_ref, used_ref, gradient_ref, out_ref, sems):
    slots = out_ref.shape[0]
    for s in range(slots):
        used = used_ref[s] > 0

        @pl.when(used)
        def _():
            pltpu.make_async_copy(gradient_ref.at[source_ref[s]], out_ref.at[s], sems.at[s]).start()

        @pl.when(jnp.logical_not(used))
        def _():
            out_ref[s] = jnp.zeros(out_ref.shape[1:], jnp.float32)

    for s in range(slots):
        @pl.when(used_ref[s] > 0)
        def _():
            pltpu.make_async_copy(gradient_ref.at[0], out_ref.at[s], sems.at[s]).wait()


def gather_blocks(gradient, source, used):
    slots = source.shape[0]
    _, rows, columns = gradient.shape
    smem = pl.BlockSpec(memory_space=pltpu.SMEM)
    hbm = pl.BlockSpec(memory_space=pl.ANY)
    return pl.pallas_call(
        gather_kernel,
        in_specs=[smem, smem, hbm],
        out_specs=pl.BlockSpec(memory_space=pltpu.VMEM),
        out_shape=jax.ShapeDtypeStruct((slots, rows, columns), jnp.float32),
        scratch_shapes=[pltpu.SemaphoreType.DMA((slots,))],
        compiler_params=pltpu.CompilerParams(vmem_limit_bytes=56 * 2**20),
    )(source, used, gradient)


def halves(value):
    high = value.astype(jnp.bfloat16)
    low = (value - high.astype(jnp.float32)).astype(jnp.bfloat16)
    return high, low


def put_left(ref, rows, value):
    n = ref.shape[1] // 3
    high, low = halves(value)
    ref[rows, 0:n] = high
    ref[rows, n : 2 * n] = high
    ref[rows, 2 * n : 3 * n] = low


def put_right(ref, start, count, value):
    n = ref.shape[0] // 3
    high, low = halves(value)
    ref[pl.ds(start, count), :] = high
    ref[pl.ds(n + start, count), :] = low
    ref[pl.ds(2 * n + start, count), :] = high


def chunks(n, body):
    @pl.loop(0, n // ROWS)
    def _(index):
        start = pl.multiple_of(index * ROWS, ROWS)
        body(start, pl.ds(start, ROWS))


def dot(left, rows, right):
    return jnp.dot(left[rows, :], right[...], preferred_element_type=jnp.float32)


def eye_part(start, n):
    row = lax.broadcasted_iota(jnp.int32, (ROWS, n), 0) + start
    return row == lax.broadcasted_iota(jnp.int32, (ROWS, n), 1)


def new_factor(state, left, right, total, n):
    total[...] = jnp.zeros_like(total)

    def part(start, rows):
        value = factor_decay * state[rows, :] + (1.0 - factor_decay) * dot(left, rows, right)
        state[rows, :] = value
        shifted = value + jnp.where(eye_part(start, n), root_eps, 0.0)
        square = jnp.sum(shifted * shifted, axis=0, keepdims=True)
        total[...] += jnp.broadcast_to(jnp.sum(square, axis=1, keepdims=True), total.shape)

    chunks(n, part)


def inverse_root(state, total, left, right, one, two, emit, n):
    scale = jnp.sqrt(total[0:1, 0:1])
    coefficient = lax.rsqrt(jnp.sqrt(scale))
    inverse = 1.0 / scale

    def first(start, rows):
        value = (state[rows, :] + jnp.where(eye_part(start, n), root_eps, 0.0)) * inverse
        one[rows, :] = value
        put_left(left, rows, value)
        put_right(right, start, ROWS, value)

    chunks(n, first)

    def second(start, rows):
        two[rows, :] = dot(left, rows, right)

    chunks(n, second)

    def split_second(start, rows):
        put_right(right, start, ROWS, two[rows, :])

    chunks(n, split_second)

    def third(start, rows):
        cube = dot(left, rows, right)
        m, m2 = one[rows, :], two[rows, :]
        one[rows, :] = jnp.where(eye_part(start, n), ROOT[0], 0.0) + ROOT[1] * m + ROOT[2] * m2 + ROOT[3] * cube
        two[rows, :] = ROOT[4] * m + ROOT[5] * m2 + ROOT[6] * cube
        put_left(left, rows, cube)

    chunks(n, third)

    def split_third(start, rows):
        put_right(right, start, ROWS, two[rows, :])

    chunks(n, split_third)

    def last(start, rows):
        emit(start, rows, coefficient * (one[rows, :] + dot(left, rows, right)))

    chunks(n, last)


def step_kernel(
    n_dp, n_t, near,
    target_ref, out_ref, gradient_hbm, second_hbm, momentum_hbm, left_hbm, right_hbm,
    direction_out, moment_out, left_out, right_out,
    gradient, second, momentum, ret_ref, adam_ref, adam_all, sum_all,
    stage, gbuf, lbuf, rbuf, pbuf, psum, total, one, two,
    g_left, g_right, gt_left, gt_right, w_left, w_right, x_left, x_right,
    s1, r1, s2, r2, s3, r3, s4, r4, s5, r5, lsem, rsem, losem, rosem, fsem, dsem, msem,
):
    i = lax.axis_index("dp")
    t = lax.axis_index("tensor")
    rows = out_ref.shape[2]
    n = lbuf.shape[1]
    slots = 2 * near

    def load(index):
        return (
            pltpu.make_async_copy(left_hbm.at[index], lbuf.at[index], lsem.at[index]),
            pltpu.make_async_copy(right_hbm.at[index], rbuf.at[index], rsem.at[index]),
        )

    def save(index):
        return (
            pltpu.make_async_copy(lbuf.at[index], left_out.at[index], losem.at[index]),
            pltpu.make_async_copy(rbuf.at[index], right_out.at[index], rosem.at[index]),
        )

    barrier = pltpu.get_barrier_semaphore()
    for a in range(n_dp):
        for b in range(n_t):
            @pl.when(jnp.logical_not((i == a) & (t == b)))
            def _():
                pl.semaphore_signal(barrier, inc=1, device_id=(a, b), device_id_type=MESH)
    pl.semaphore_wait(barrier, n_dp * n_t - 1)

    def spread(r, step):
        other = lax.rem(i + step, n_dp)
        return pltpu.make_async_remote_copy(
            src_ref=out_ref.at[other, r], dst_ref=stage.at[r, i],
            send_sem=s1.at[r, step], recv_sem=r1.at[r, i],
            device_id=(other, t), device_id_type=MESH,
        )

    def forward(r, j):
        return pltpu.make_async_remote_copy(
            src_ref=stage.at[r, j], dst_ref=gbuf.at[r, lax.rem(j, near), t],
            send_sem=s2.at[r, j], recv_sem=r2.at[r, lax.rem(j, near), t],
            device_id=(i, j // near), device_id_type=MESH,
        )

    def forward_here(r, j):
        return pltpu.make_async_copy(
            stage.at[r, j], gbuf.at[r, lax.rem(j, near), t], r2.at[r, lax.rem(j, near), t]
        )

    def own(r):
        return pltpu.make_async_copy(out_ref.at[i, r], stage.at[r, i], r1.at[r, i])

    def adam_copy(step):
        return pltpu.make_async_remote_copy(
            src_ref=adam_ref, dst_ref=adam_all.at[t],
            send_sem=s5.at[step], recv_sem=r5.at[t],
            device_id=(i, lax.rem(t + step, n_t)), device_id_type=MESH,
        )

    adam_here = pltpu.make_async_copy(adam_ref, adam_all.at[t], r5.at[t])

    def home(r, b, q):
        return pltpu.make_async_remote_copy(
            src_ref=pbuf.at[r, b, pl.ds(pl.multiple_of(q * rows, rows), rows)], dst_ref=ret_ref.at[i, r],
            send_sem=s3.at[r, b, q], recv_sem=r3.at[r, i],
            device_id=(t * near + b, q), device_id_type=MESH,
        )

    def home_here(r, b, q):
        return pltpu.make_async_copy(
            pbuf.at[r, b, pl.ds(pl.multiple_of(q * rows, rows), rows)], ret_ref.at[i, r], r3.at[r, i]
        )

    def home_sum(r, b, q):
        return pltpu.make_async_remote_copy(
            src_ref=psum.at[r, b], dst_ref=sum_all.at[i, r],
            send_sem=s4.at[r, b, q], recv_sem=r4.at[r, i],
            device_id=(t * near + b, q), device_id_type=MESH,
        )

    def home_sum_here(r, b, q):
        return pltpu.make_async_copy(psum.at[r, b], sum_all.at[i, r], r4.at[r, i])

    for r in range(2):
        own(r).start()
        for step in range(1, n_dp):
            spread(r, step).start()
    fetch = [
        pltpu.make_async_copy(gradient_hbm, gradient, fsem.at[0]),
        pltpu.make_async_copy(second_hbm, second, fsem.at[1]),
        pltpu.make_async_copy(momentum_hbm, momentum, fsem.at[2]),
    ]
    for copy in fetch:
        copy.start()
    for index in range(slots):
        for copy in load(index):
            copy.start()

    blocks = gradient.shape[0]

    def block_moment(k):
        return pltpu.make_async_copy(second.at[k], moment_out.at[k], msem.at[k])

    def block_direction(k):
        return pltpu.make_async_copy(momentum.at[k], direction_out.at[k], dsem.at[k])

    for r in range(2):
        if r == 1:
            fetch[0].wait()
            fetch[1].wait()

            @pl.loop(0, blocks)
            def _(k):
                value = gradient[k]
                moment = adam_decay * second[k] + (1.0 - adam_decay) * value * value
                second[k] = moment
                adam = value / (jnp.sqrt(moment) + adam_eps)
                square = jnp.sum(adam * adam, axis=0, keepdims=True)
                adam_ref[k] = jnp.broadcast_to(jnp.sum(square, axis=1, keepdims=True), adam_ref.shape[1:])
                block_moment(k).start()

            adam_here.start()
            for step in range(1, n_t):
                adam_copy(step).start()
        for step in range(n_dp):
            j = lax.rem(i + n_dp - step, n_dp)
            pltpu.make_async_copy(stage.at[r, j], stage.at[r, j], r1.at[r, j]).wait()
            same = j // near == t

            @pl.when(same)
            def _():
                forward_here(r, j).start()

            @pl.when(jnp.logical_not(same))
            def _():
                forward(r, j).start()

    @pl.loop(0, slots)
    def _(q):
        r = q // near
        b = lax.rem(q, near)
        index = b * 2 + r
        for copy in load(index):
            copy.wait()
        for part in range(n_t):
            pltpu.make_async_copy(gbuf.at[r, b, part], gbuf.at[r, b, part], r2.at[r, b, part]).wait()
        left, right = lbuf.at[index], rbuf.at[index]
        for part in range(n_t):
            here = pl.ds(part * rows, rows)
            value = gbuf[r, b, part]
            put_left(g_left, here, value)
            put_right(g_right, part * rows, rows, value)
            one[here, :] = value

        def turn(start, here):
            value = jnp.transpose(one[:, here])
            put_left(gt_left, here, value)
            put_right(gt_right, start, ROWS, value)

        for start in range(0, n, ROWS):
            turn(start, pl.ds(start, ROWS))
        new_factor(left, g_left, gt_right, total.at[0], n)
        new_factor(right, gt_left, g_right, total.at[1], n)
        for copy in save(index):
            copy.start()

        def keep_left(start, here, value):
            put_left(x_left, here, value)

        def keep_right(start, here, value):
            put_right(x_right, start, ROWS, value)

        inverse_root(left, total.at[0], w_left, w_right, one, two, keep_left, n)
        inverse_root(right, total.at[1], w_left, w_right, one, two, keep_right, n)

        def middle(start, here):
            put_left(w_left, here, dot(x_left, here, g_right))

        chunks(n, middle)
        psum[r, b] = jnp.zeros(psum.shape[2:], jnp.float32)

        def final(start, here):
            value = dot(w_left, here, x_right)
            pbuf[r, b, here, :] = value
            square = jnp.sum(value * value, axis=0, keepdims=True)
            psum[r, b] += jnp.broadcast_to(jnp.sum(square, axis=1, keepdims=True), psum.shape[2:])

        chunks(n, final)
        for part in range(n_t):
            mine = (t * near + b == i) & (t == part)

            @pl.when(mine)
            def _():
                home_here(r, b, part).start()
                home_sum_here(r, b, part).start()

            @pl.when(jnp.logical_not(mine))
            def _():
                home(r, b, part).start()
                home_sum(r, b, part).start()

    fetch[2].wait()
    for r in range(2):
        for step in range(1, n_dp):
            spread(r, step).wait_send()
        for j in range(n_dp):
            @pl.when(j // near != t)
            def _():
                forward(r, j).wait_send()
    for step in range(1, n_t):
        adam_copy(step).wait_send()
    for index in range(slots):
        for copy in save(index):
            copy.wait()
    for part in range(n_t):
        pltpu.make_async_copy(adam_all.at[part], adam_all.at[part], r5.at[part]).wait()
    for r in range(2):
        for b in range(near):
            for part in range(n_t):
                @pl.when(jnp.logical_not((t * near + b == i) & (t == part)))
                def _():
                    home(r, b, part).wait_send()
                    home_sum(r, b, part).wait_send()
        for o in range(n_dp):
            pltpu.make_async_copy(ret_ref.at[o, r], ret_ref.at[o, r], r3.at[r, o]).wait()
            pltpu.make_async_copy(sum_all.at[o, r], sum_all.at[o, r], r4.at[r, o]).wait()

    area = float(n * n)

    @pl.loop(0, blocks)
    def _(k):
        target = target_ref[k]
        other, r = target // 2, lax.rem(target, 2)
        adam_sum = adam_all[0, k]
        for part in range(1, n_t):
            adam_sum = adam_sum + adam_all[part, k]
        ratio = jnp.sqrt(adam_sum / area / (sum_all[other, r] / area + mean_eps))
        momentum[k] = momentum_decay * momentum[k] + ratio[0:1, 0:1] * ret_ref[other, r]
        block_direction(k).start()

    @pl.loop(0, blocks)
    def _(k):
        block_moment(k).wait()
        block_direction(k).wait()


def step(target, outgoing, gradient, second, momentum, left_old, right_old, n_dp, n_t):
    near = n_dp // n_t
    slots = 2 * near
    _, _, rows, n = outgoing.shape
    blocks = gradient.shape[0]
    f32, bf16 = jnp.float32, jnp.bfloat16
    hbm = pl.BlockSpec(memory_space=pl.ANY)
    dma = pltpu.SemaphoreType.DMA
    wide, tall = pltpu.VMEM((n, 3 * n), bf16), pltpu.VMEM((3 * n, n), bf16)
    return pl.pallas_call(
        functools.partial(step_kernel, n_dp, n_t, near),
        out_shape=(
            jax.ShapeDtypeStruct(gradient.shape, f32),
            jax.ShapeDtypeStruct(gradient.shape, f32),
            jax.ShapeDtypeStruct((slots, n, n), f32),
            jax.ShapeDtypeStruct((slots, n, n), f32),
        ),
        in_specs=[pl.BlockSpec(memory_space=pltpu.SMEM)] + [hbm] * 6,
        out_specs=(hbm, hbm, hbm, hbm),
        scratch_shapes=[
            pltpu.VMEM(gradient.shape, f32),
            pltpu.VMEM(gradient.shape, f32),
            pltpu.VMEM(gradient.shape, f32),
            pltpu.VMEM((n_dp, 2, rows, n), f32),
            pltpu.VMEM((blocks, 8, 128), f32),
            pltpu.VMEM((n_t, blocks, 8, 128), f32),
            pltpu.VMEM((n_dp, 2, 8, 128), f32),
            pltpu.VMEM((2, n_dp, rows, n), f32),
            pltpu.VMEM((2, near, n_t, rows, n), f32),
            pltpu.VMEM((slots, n, n), f32),
            pltpu.VMEM((slots, n, n), f32),
            pltpu.VMEM((2, near, n, n), f32),
            pltpu.VMEM((2, near, 8, 128), f32),
            pltpu.VMEM((2, 8, 128), f32),
            pltpu.VMEM((n, n), f32),
            pltpu.VMEM((n, n), f32),
            wide, tall, wide, tall, wide, tall, wide, tall,
            dma((2, n_dp)), dma((2, n_dp)),
            dma((2, n_dp)), dma((2, near, n_t)),
            dma((2, near, n_t)), dma((2, n_dp)),
            dma((2, near, n_t)), dma((2, n_dp)),
            dma((n_t,)), dma((n_t,)),
            dma((slots,)), dma((slots,)), dma((slots,)), dma((slots,)),
            dma((3,)), dma((blocks,)), dma((blocks,)),
        ],
        compiler_params=pltpu.CompilerParams(
            collective_id=0, has_side_effects=True, vmem_limit_bytes=56 * 2**20
        ),
    )(target, outgoing, gradient, second, momentum, left_old, right_old)


def per_device(gradient, second_moment, momentum, left_state, right_state, owner):
    dp_count = lax.axis_size("dp")
    tensor_count = lax.axis_size("tensor")
    blocks_here, rows, columns = gradient.shape
    slots_dp = PAIR_MOST * dp_count
    owners = owner[:, 0]
    position = jnp.arange(blocks_here, dtype=jnp.int32)
    earlier = (owners[:, None] == owners[None, :]) & (position[None, :] < position[:, None])
    rank = jnp.sum(earlier.astype(jnp.int32), axis=1)
    target = owners * PAIR_MOST + rank
    select = (target[None, :] == jnp.arange(slots_dp, dtype=jnp.int32)[:, None]).astype(jnp.int32)
    source = jnp.sum(select * position[None, :], axis=1)
    used = jnp.sum(select, axis=1)
    outgoing = gather_blocks(gradient, source, used).reshape(dp_count, PAIR_MOST, rows, columns)
    direction, moment_new, left_new, right_new = step(
        target, outgoing, gradient, second_moment, momentum, left_state[0], right_state[0],
        dp_count, tensor_count,
    )
    return (direction, moment_new, left_new[None], right_new[None])


def solution(mesh):
    return jax.shard_map(
        per_device,
        mesh=mesh,
        in_specs=(
            P("dp", "tensor", None),
            P("dp", "tensor", None),
            P("dp", "tensor", None),
            P("dp", "tensor", None, None),
            P("dp", "tensor", None, None),
            P("dp", None),
        ),
        out_specs=(
            P("dp", "tensor", None),
            P("dp", "tensor", None),
            P("dp", "tensor", None, None),
            P("dp", "tensor", None, None),
        ),
        check_vma=False,
    )
```
